256 devices in a mesh: dp: 32 (over x_lo, z, core), tensor: 8 (over y, x_hi).
Axes of the slice: x: 4 (x_hi: 2, x_lo: 2; x = x_hi * 2 + x_lo), y: 4, z: 8, core: 2. Of those that a mesh axis runs over, the one named last changes fastest.
Arguments:
- clips: bfloat16 [32, 8, 8, 16, 1024], P('dp', None, None, None, 'tensor'), may hold values from -6 to 6
- out_grad: bfloat16 [32, 8, 8, 16, 1024], P('dp', None, None, None, 'tensor'), may hold values from -6 to 6
- spatial_weight: bfloat16 [3, 3, 1024, 1024], P(None, None, None, 'tensor'), may hold values from -0.0625 to 0.0625
- temporal_weight: bfloat16 [3, 1024, 1024], P(None, 'tensor'), may hold values from -0.109375 to 0.109375
Outputs:
- mixed: bfloat16 [32, 8, 8, 16, 1024], P('dp', None, None, None, 'tensor')
- clip_grad: bfloat16 [32, 8, 8, 16, 1024], P('dp', None, None, None, 'tensor')
- spatial_grad: bfloat16 [3, 3, 1024, 1024], P(None, None, 'dp', 'tensor')
- temporal_grad: bfloat16 [3, 1024, 1024], P(None, 'tensor', 'dp')
The draws below stay inside these ranges and needn't reach their ends.
All inputs are finite; a program needn't handle non-finite values.
Results may differ from the reference program's by a relative error of at most 0.006.
Values may be sent and summed in bfloat16 or wider, within the bound.
No kernel may reach another device: no remote copies, remote signals or barrier semaphores. Data moves between devices by JAX's collectives and lax.ppermute only.
A program may use at most 128 MiB of HBM per device.

```python
import jax
import jax.numpy as jnp
from jax import lax

C = 1024
GS = 32
FRAMES = 8
HEIGHT = 8
BREADTH = 16
CLIPS = 32
POSITIONS = 32768


def with_spikes(entries, key, source, target, parts, factor):
    owner, partner = [(jnp.arange(entries.shape[dim]) // (entries.shape[dim] // parts)).reshape([-1 if axis == dim else 1 for axis in range(entries.ndim)]) for dim in (source, target)]
    chosen = jax.random.permutation(key, parts)[partner]
    strong = (owner == chosen) | (owner == (partner + parts // 2) % parts)
    return jnp.where(strong, factor * entries, entries)


def levels(rng, shape, cuts, least, top_value):
    def one(axis_at, blocks):
        steps = jax.random.uniform(jax.random.fold_in(jax.random.fold_in(rng, 6), axis_at), (blocks,), jnp.float32, least / len(cuts), top_value / len(cuts))
        return jnp.repeat(jnp.exp(steps), shape[axis_at] // blocks).reshape((-1,) + (1,) * (len(shape) - axis_at - 1))

    gain = one(*cuts[0])
    for cut in cuts[1:]:
        gain = gain * one(*cut)
    return gain


def noise(key, extent, deviation, most, split=(), held_as=jnp.bfloat16):
    values = deviation * jax.random.normal(key, extent, jnp.float32)
    if split:
        values = values * levels(key, extent, split, -0.22, 0.18)
    return jnp.clip(values, -most, most).astype(held_as)


def noise_with(rng, shape, deviation, reach, cuts, heavy, held_as=jnp.bfloat16):
    entries = deviation * jax.random.normal(rng, shape, jnp.float32)
    if cuts:
        entries = entries * levels(rng, shape, cuts, -0.22, 0.18)
    return jnp.clip(with_spikes(entries, jax.random.fold_in(rng, 3), *heavy), -reach, reach).astype(held_as)


def setup_inputs(seed: int = 0) -> dict:
    keys = jax.random.split(jax.random.key(seed), 5)
    clips = noise_with(keys[0], (CLIPS, FRAMES, HEIGHT, BREADTH, C), 1.0, 6.0, ((0, 32), (4, 8)), (0, 4, 32, 2.75))
    out_grad = noise_with(keys[1], (CLIPS, FRAMES, HEIGHT, BREADTH, C), 1.0, 6.0, ((0, 32), (4, 8)), (0, 4, 32, 2.75))
    spatial_weight = noise(keys[2], (3, 3, C, C), (9 * C) ** -0.5, 0.0625, ((3, 8),))
    temporal_weight = noise(keys[3], (3, C, C), (3 * C) ** -0.5, 0.109375, ((1, 8),))
    return {"clips": clips, "out_grad": out_grad, "spatial_weight": spatial_weight, "temporal_weight": temporal_weight}


def group_silu(values):
    shaped = values.reshape(values.shape[0], -1, values.shape[-1] // GS, GS)
    center = lax.optimization_barrier(jnp.mean(shaped, axis=(1, 3), keepdims=True))
    offsets = shaped - center
    spread = lax.optimization_barrier(jnp.mean(offsets * offsets, axis=(1, 3), keepdims=True))
    return jax.nn.silu(offsets * lax.rsqrt(spread + 1e-05)).reshape(values.shape)

def spatial_conv(inputs, kernel):
    dims = inputs.shape
    flat = inputs.reshape((dims[0] * dims[1], dims[2], dims[3], dims[4]))
    result = lax.conv_general_dilated(flat, kernel, (1, 1), ((1, 1), (1, 1)), dimension_numbers=('NHWC', 'HWIO', 'NHWC'), preferred_element_type=jnp.float32)
    return result.reshape(dims[:4] + (kernel.shape[3],))

def flipped(kernel):
    return jnp.transpose(kernel[::-1, ::-1], (0, 1, 3, 2))

def spatial_wgrad(inputs, grads):
    dims = inputs.shape
    padded = jnp.pad(inputs, ((0, 0), (0, 0), (1, 1), (1, 1), (0, 0)))
    right_side = grads.reshape(-1, grads.shape[-1])
    collected = []
    for row_tap in range(3):
        for col_tap in range(3):
            window = padded[:, :, row_tap:row_tap + dims[2], col_tap:col_tap + dims[3]].reshape(-1, dims[4])
            collected.append(lax.dot_general(window, right_side, (((0,), (0,)), ((), ())), preferred_element_type=jnp.float32))
    return jnp.stack(collected).reshape(3, 3, dims[4], grads.shape[-1])

def temporal_conv(inputs, kernel):
    frame_count = inputs.shape[1]
    padded = jnp.pad(inputs, ((0, 0), (1, 1), (0, 0), (0, 0), (0, 0)))
    result = jnp.zeros((inputs.size // inputs.shape[-1], kernel.shape[2]), jnp.float32)
    for kernel_tap in range(3):
        window = padded[:, kernel_tap:kernel_tap + frame_count].reshape(-1, inputs.shape[-1])
        result = result + jnp.dot(window, kernel[kernel_tap], preferred_element_type=jnp.float32)
    return result.reshape(inputs.shape[:4] + (kernel.shape[2],))

def temporal_back(grads, kernel):
    frame_count = grads.shape[1]
    padded = jnp.pad(grads, ((0, 0), (1, 1), (0, 0), (0, 0), (0, 0)))
    result = jnp.zeros((grads.size // grads.shape[-1], kernel.shape[1]), jnp.float32)
    for kernel_tap in range(3):
        window = padded[:, 2 - kernel_tap:2 - kernel_tap + frame_count].reshape(-1, grads.shape[-1])
        result = result + lax.dot_general(window, kernel[kernel_tap], (((1,), (1,)), ((), ())), preferred_element_type=jnp.float32)
    return result.reshape(grads.shape[:4] + (kernel.shape[1],))

def temporal_wgrad(inputs, grads):
    frame_count = inputs.shape[1]
    padded = jnp.pad(inputs, ((0, 0), (1, 1), (0, 0), (0, 0), (0, 0)))
    right_side = grads.reshape(-1, grads.shape[-1])
    collected = []
    for kernel_tap in range(3):
        window = padded[:, kernel_tap:kernel_tap + frame_count].reshape(-1, inputs.shape[-1])
        collected.append(lax.dot_general(window, right_side, (((0,), (0,)), ((), ())), preferred_element_type=jnp.float32))
    return jnp.stack(collected)

def reference(clips, out_grad, spatial_weight, temporal_weight):
    grad_scale = 1.0 / jnp.sqrt(jnp.float32(POSITIONS))
    first_act, pull_first = jax.vjp(group_silu, clips.astype(jnp.float32))
    hidden_first = first_act.astype(jnp.bfloat16)
    spatial_out = spatial_conv(hidden_first, spatial_weight)
    second_act, pull_second = jax.vjp(group_silu, spatial_out)
    hidden_second = second_act.astype(jnp.bfloat16)
    mixed = (clips.astype(jnp.float32) + temporal_conv(hidden_second, temporal_weight)).astype(jnp.bfloat16)
    grad_second = temporal_back(out_grad, temporal_weight)
    grad_spatial = pull_second(grad_second)[0].astype(jnp.bfloat16)
    temporal_grad = (temporal_wgrad(hidden_second, out_grad) * grad_scale).astype(jnp.bfloat16)
    grad_first = spatial_conv(grad_spatial, flipped(spatial_weight))
    spatial_grad = (spatial_wgrad(hidden_first, grad_spatial) * grad_scale).astype(jnp.bfloat16)
    clip_grad = (out_grad.astype(jnp.float32) + pull_first(grad_first)[0]).astype(jnp.bfloat16)
    return (mixed, clip_grad, spatial_grad, temporal_grad)
```

```python
import jax
import jax.numpy as jnp
from jax import lax
from jax.sharding import PartitionSpec as P

GS = 32
BF = jnp.bfloat16
F32 = jnp.float32
Y_GROUPS = [[y * 2 + h for y in range(4)] for h in range(2)]
X_GROUPS = [[2 * y, 2 * y + 1] for y in range(4)]
CORE_GROUPS = [[2 * k, 2 * k + 1] for k in range(16)]
XLO_GROUPS = [[k, k + 16] for k in range(16)]
Z_GROUPS = [[l * 16 + z * 2 + c for z in range(8)] for l in range(2) for c in range(2)]


def swap(values, axis, groups):
    return lax.all_to_all(
        values, axis, split_axis=0, concat_axis=0, tiled=True, axis_index_groups=groups
    )


def over_y(values):
    return swap(values, "tensor", Y_GROUPS)


def over_x(values):
    return swap(values, "tensor", X_GROUPS)


def group_mean(values):
    lanes = jnp.sum(values, axis=0).reshape(-1, GS)
    means = jnp.sum(lanes, axis=1, keepdims=True) / (values.shape[0] * GS)
    return jnp.broadcast_to(means, lanes.shape).reshape(1, -1)


def normalize(values):
    offsets = values - group_mean(values)
    scale = lax.rsqrt(group_mean(offsets * offsets) + 1e-05)
    return offsets * scale, scale


def act(unit):
    return unit * jax.nn.sigmoid(unit)


def act_back(unit, scale, grads):
    gate = jax.nn.sigmoid(unit)
    inner = grads * (gate * (1.0 + unit * (1.0 - gate)))
    return scale * (inner - group_mean(inner) - unit * group_mean(inner * unit))


def conv(inputs, kernel):
    return lax.conv_general_dilated(
        inputs.reshape(8, 8, 16, -1),
        kernel,
        (1, 1),
        ((1, 1), (1, 1)),
        dimension_numbers=("NHWC", "HWIO", "NHWC"),
        preferred_element_type=F32,
    ).reshape(1024, -1)


def shifts(values):
    padded = jnp.pad(values.reshape(8, 8, 16, -1), ((0, 0), (1, 1), (1, 1), (0, 0)))
    return [
        padded[:, a : a + 8, b : b + 16].reshape(1024, -1) for a in (2, 1, 0) for b in (2, 1, 0)
    ]


def frame_shifts(values):
    padded = jnp.pad(values, ((128, 128), (0, 0)))
    return [padded[128 * k : 128 * k + 1024] for k in range(3)]


def tdot(left, right):
    return lax.dot_general(left, right, (((0,), (0,)), ((), ())), preferred_element_type=F32)


def wide(parts):
    return jnp.concatenate(list(parts), axis=1)


def per_device(clips, out_grad, spatial_weight, temporal_weight):
    tensor, data = lax.axis_index("tensor"), lax.axis_index("dp")
    x_hi, core = tensor % 2, data % 2
    z_mid = (data // 4) % 2
    grad_scale = 1.0 / jnp.sqrt(jnp.float32(32768))
    grads = out_grad.reshape(1024, 128)
    grads_all = over_y(jnp.broadcast_to(grads, (4, 1024, 128)).reshape(4096, 128))
    grads_all = wide(grads_all.reshape(4, 1024, 128))

    spatial_split = spatial_weight.reshape(9, 4, 2, 128, 128)
    temporal_split = temporal_weight.reshape(3, 128, 4, 2, 128)
    spatial_keep = lax.dynamic_index_in_dim(spatial_split, x_hi, 2, False)
    temporal_keep = lax.dynamic_index_in_dim(temporal_split, x_hi, 3, False)
    spatial_give = lax.dynamic_index_in_dim(spatial_split, 1 - x_hi, 2, False)
    temporal_give = lax.dynamic_index_in_dim(temporal_split, 1 - x_hi, 3, False)
    spatial_give = lax.dynamic_slice_in_dim(spatial_give, 2 * core, 2, 1)
    temporal_give = lax.dynamic_slice_in_dim(temporal_give, 2 * core, 2, 2)
    temporal_give = jnp.moveaxis(temporal_give, 2, 1)
    packed = jnp.concatenate([spatial_give.reshape(-1, 128), temporal_give.reshape(-1, 128)])
    cross = []
    for d in range(32):
        for t in range(8):
            cross.append((d * 8 + t, ((d + 16) % 32) * 8 + (t ^ 1)))
    packed = lax.ppermute(packed, ("dp", "tensor"), cross)
    rows = packed.shape[0]
    packed = swap(jnp.broadcast_to(packed, (2, rows, 128)).reshape(-1, 128), "dp", CORE_GROUPS)
    packed = packed.reshape(2, rows, 128)
    spatial_got = packed[:, : 9 * 256].reshape(2, 9, 2, 128, 128)
    spatial_got = jnp.moveaxis(spatial_got, 0, 1).reshape(9, 512, 128)
    temporal_got = packed[:, 9 * 256 :].reshape(2, 3, 2, 128, 128)
    temporal_got = jnp.moveaxis(temporal_got, (0, 1, 2, 3, 4), (2, 0, 3, 1, 4)).reshape(3, 128, 512)
    first = x_hi == 0
    spatial_keep = spatial_keep.reshape(9, 512, 128)
    temporal_keep = temporal_keep.reshape(3, 128, 512)
    spatial = jnp.concatenate(
        [jnp.where(first, spatial_keep, spatial_got), jnp.where(first, spatial_got, spatial_keep)], 2
    )
    temporal = jnp.concatenate(
        [
            jnp.where(first, temporal_keep, temporal_got),
            jnp.where(first, temporal_got, temporal_keep),
        ],
        1,
    )

    clip_rows = clips.reshape(1024, 128).astype(F32)
    unit_first, scale_first = normalize(clip_rows)
    hidden_first = act(unit_first).astype(BF)
    first_all = over_y(jnp.broadcast_to(hidden_first, (4, 1024, 128)).reshape(4096, 128))
    first_all = wide(first_all.reshape(4, 1024, 128))

    second_part = sum(
        lax.dot_general(w, temporal[2 - k], (((1,), (1,)), ((), ())), preferred_element_type=F32)
        for k, w in enumerate(frame_shifts(grads_all))
    )
    second_part = second_part.astype(BF).reshape(1024, 2, 128).swapaxes(0, 1)
    second_part = over_x(second_part.reshape(2048, 128)).reshape(2, 1024, 128)
    grad_second = second_part[0].astype(F32) + second_part[1].astype(F32)

    spatial_part = conv(first_all, spatial.reshape(3, 3, 512, 256))
    spatial_part = spatial_part.astype(BF).reshape(1024, 2, 128).swapaxes(0, 1)
    spatial_part = over_x(spatial_part.reshape(2048, 128)).reshape(2, 1024, 128)
    spatial_out = spatial_part[0].astype(F32) + spatial_part[1].astype(F32)

    unit_second, scale_second = normalize(spatial_out)
    hidden_second = act(unit_second).astype(BF)
    grad_spatial = act_back(unit_second, scale_second, grad_second).astype(BF)
    both = jnp.stack([hidden_second, grad_spatial])
    both = over_x(jnp.broadcast_to(both, (2, 2, 1024, 128)).reshape(-1, 128))
    both = both.reshape(2, 2, 1024, 128)
    second_all = wide(both[:, 0])
    spatial_grads = wide(both[:, 1])

    shifted = jnp.concatenate(shifts(spatial_grads), axis=1)
    shifted_second = jnp.concatenate(frame_shifts(second_all), axis=1)
    spatial_local = tdot(first_all, shifted)
    temporal_local = tdot(grads_all, shifted_second)
    local = jnp.concatenate([spatial_local, temporal_local], axis=1)
    local = local.astype(BF).reshape(2, 2, 2, 2, 32, 12, 2, 128)
    local = local.transpose(3, 0, 1, 6, 2, 5, 4, 7)
    local = swap(local.reshape(-1, 128), "dp", CORE_GROUPS).reshape(2, -1, 128)
    local = (local[0].astype(F32) + local[1].astype(F32)).astype(BF)
    local = swap(local, "dp", XLO_GROUPS).reshape(2, -1, 128)
    local = (local[0].astype(F32) + local[1].astype(F32)).astype(BF)
    local = swap(local, "dp", Z_GROUPS).reshape(8, 12 * 32, 128)
    share = (jnp.sum(local.astype(F32), axis=0) * grad_scale).astype(BF)
    move = []
    for d in range(32):
        for t in range(8):
            if (d // 4) % 2 != t % 2:
                move.append((d * 8 + t, (d ^ 4) * 8 + (t ^ 1)))
    moved = lax.ppermute(share, ("dp", "tensor"), move)
    share = jnp.where(z_mid == x_hi, share, moved).reshape(12, 32, 128)
    spatial_share = share[:9].reshape(3, 3, 32, 128)
    temporal_share = share[9:].swapaxes(1, 2)

    temporal_part = sum(
        jnp.dot(w, temporal[k], preferred_element_type=F32)
        for k, w in enumerate(frame_shifts(second_all))
    )
    temporal_part = temporal_part.astype(BF).reshape(1024, 4, 128).swapaxes(0, 1)
    temporal_part = over_y(temporal_part.reshape(4096, 128)).reshape(4, 1024, 128)
    mixed = (clip_rows + jnp.sum(temporal_part.astype(F32), axis=0)).astype(BF)

    first_part = lax.dot_general(
        shifted,
        spatial.swapaxes(1, 2).reshape(9 * 256, 512),
        (((1,), (0,)), ((), ())),
        preferred_element_type=F32,
    )
    first_part = first_part.astype(BF).reshape(1024, 4, 128).swapaxes(0, 1)
    first_part = over_y(first_part.reshape(4096, 128)).reshape(4, 1024, 128)
    grad_first = jnp.sum(first_part.astype(F32), axis=0)
    clip_grad = (grads.astype(F32) + act_back(unit_first, scale_first, grad_first)).astype(BF)
    return (
        mixed.reshape(clips.shape),
        clip_grad.reshape(clips.shape),
        spatial_share,
        temporal_share,
    )


def solution(mesh):
    placed = (
        P("dp", None, None, None, "tensor"),
        P("dp", None, None, None, "tensor"),
        P(None, None, None, "tensor"),
        P(None, "tensor", None),
    )
    return jax.shard_map(
        per_device,
        mesh=mesh,
        in_specs=placed,
        out_specs=(
            P("dp", None, None, None, "tensor"),
            P("dp", None, None, None, "tensor"),
            P(None, None, "dp", "tensor"),
            P(None, "tensor", "dp"),
        ),
        check_vma=False,
    )
```

```python
import jax
import jax.numpy as jnp
from jax import lax
from jax.experimental import pallas as pl
from jax.experimental.pallas import tpu as pltpu
from jax.sharding import PartitionSpec as P

GS = 32
ROWS = 1024
BF = jnp.bfloat16
F32 = jnp.float32
NT = (((1,), (1,)), ((), ()))
Z_GROUPS = [[l * 16 + z * 2 + c for z in range(8)] for l in range(2) for c in range(2)]


def tensor_move(values, y_step, x_flip):
    pairs = [(t, ((t // 2 + y_step) % 4) * 2 + (t % 2 ^ x_flip)) for t in range(8)]
    return lax.ppermute(values, "tensor", pairs)


def data_move(values, bits):
    return lax.ppermute(values, "dp", [(d, d ^ bits) for d in range(32)])


def block(index):
    return pl.ds(pl.multiple_of(index * 128, 128), 128)


def call(body, outs, scratch, args, flops, name, unread=0):
    total = sum(a.size * a.dtype.itemsize for a in args)
    total += sum(o.size * o.dtype.itemsize for o in outs)
    smem = pl.BlockSpec(memory_space=pltpu.SMEM)
    vmem = pl.BlockSpec(memory_space=pltpu.VMEM)
    specs = [smem if a.dtype == jnp.int32 else vmem for a in args]
    if unread:
        specs[-unread:] = [pl.BlockSpec(memory_space=pl.ANY)] * unread
    result = pl.pallas_call(
        body,
        out_shape=outs,
        in_specs=specs,
        out_specs=[vmem] * len(outs),
        scratch_shapes=scratch,
        compiler_params=pltpu.CompilerParams(vmem_limit_bytes=48 * 1024 * 1024),
        cost_estimate=pl.CostEstimate(flops=flops, bytes_accessed=total, transcendentals=0),
        name=name,
    )(*args)
    return list(result)


def shape(dims, dtype):
    return jax.ShapeDtypeStruct(dims, dtype)


def group_mean(values):
    sums = jnp.sum(values, axis=0, keepdims=True)
    rows = lax.broadcasted_iota(jnp.int32, (128, 128), 0) // GS
    lanes = lax.broadcasted_iota(jnp.int32, (128, 128), 1) // GS
    same = (rows == lanes).astype(F32)
    sums = jnp.broadcast_to(sums, (8, 128))
    sums = jnp.dot(sums, same, precision=lax.Precision.HIGHEST, preferred_element_type=F32)
    return sums[0:1] * (1.0 / (ROWS * GS))


def normalize(values):
    offsets = values - group_mean(values)
    scale = lax.rsqrt(group_mean(offsets * offsets) + 1e-05)
    return offsets * scale, scale


def gate_of(unit):
    return 1.0 / (1.0 + jnp.exp(-unit))


def act_back(unit, scale, gate, grads):
    inner = grads * (gate * (1.0 + unit * (1.0 - gate)))
    return scale * (inner - group_mean(inner) - unit * group_mean(inner * unit))


def first_act_kernel(clips, after, hidden):
    unit, _ = normalize(clips[...].astype(F32))
    hidden[...] = (unit * gate_of(unit)).astype(BF)


def second_act_kernel(out_own, out_got, grad_own, grad_got, both):
    unit, scale = normalize(out_own[...] + out_got[...].astype(F32))
    gate = gate_of(unit)
    both[1] = (unit * gate).astype(BF)
    received = grad_own[...] + grad_got[...].astype(F32)
    both[0] = act_back(unit, scale, gate, received).astype(BF)


def finish_kernel(clips, out_grad, own_back, own_ahead, got_a, got_b, got_c, mixed, clip_grad):
    rows = clips[...].astype(F32)
    ahead = own_ahead[...] + got_a[1].astype(F32) + got_b[1].astype(F32) + got_c[1].astype(F32)
    mixed[...] = (rows + ahead).astype(BF)
    unit, scale = normalize(rows)
    grads = own_back[...] + got_a[0].astype(F32) + got_b[0].astype(F32) + got_c[0].astype(F32)
    back = act_back(unit, scale, gate_of(unit), grads)
    clip_grad[...] = (out_grad[...].astype(F32) + back).astype(BF)


def unfold(values, target, column, steps=(-1, 0, 1)):
    wide = values.astype(F32)
    place = lax.broadcasted_iota(jnp.int32, (ROWS, 128), 0) % 16
    for sb in (-1, 0, 1):
        moved = wide
        if sb:
            moved = pltpu.roll(wide, (-sb) % ROWS, 0)
            moved = jnp.where(place == (15 if sb == 1 else 0), 0.0, moved)
        moved = moved.astype(BF).reshape(8, 128, 128)
        zeros = jnp.zeros((8, 16, 128), BF)
        for sa in steps:
            at = column(sa, sb)
            if sa == 0:
                target[:, :, at] = moved
            elif sa == 1:
                target[:, 0:112, at] = moved[:, 16:]
                target[:, 112:128, at] = zeros
            else:
                target[:, 16:128, at] = moved[:, :112]
                target[:, 0:16, at] = zeros


def frames(values, target, column):
    zeros = jnp.zeros((128, 128), BF)
    for s in (-1, 0, 1):
        at = column(s)
        if s == 0:
            target[:, at] = values
        elif s == 1:
            target[0:896, at] = values[128:]
            target[896:1024, at] = zeros
        else:
            target[128:1024, at] = values[:896]
            target[0:128, at] = zeros


def temporal_pair(place, weight, got_a, got_b, pair):
    x_hi, core = place[1], place[2]
    for k in range(3):
        for yb in range(4):
            pair[k, 0:128, yb * 128 : yb * 128 + 128] = weight[k, :, block(2 * yb + x_hi)]
        for j in range(2):
            pair[k, 128:256, block(2 * core + j)] = got_a[k, j]
            pair[k, 128:256, block(2 - 2 * core + j)] = got_b[k, j]


def spatial_give_kernel(place, weight, give):
    x_hi, core = place[1], place[2]
    for j in range(2):
        at = block(2 * (2 * core + j) + 1 - x_hi)
        for tap in range(9):
            give[tap, j] = weight[tap, at, :]


def temporal_give_kernel(place, weight, after, give):
    x_hi, core = place[1], place[2]
    for j in range(2):
        at = block(2 * (2 * core + j) + 1 - x_hi)
        for k in range(3):
            give[k, j] = weight[k, :, at]


def spatial_pair_kernel(place, weight, got_a, got_b, pair):
    x_hi, core = place[1], place[2]
    for tap in range(9):
        for yb in range(4):
            at = tap * 512 + yb * 128
            pair[at : at + 128, 0:128] = weight[tap, block(2 * yb + x_hi), :]
        for j in range(2):
            pair[block(tap * 4 + 2 * core + j), 128:256] = got_a[tap, j]
            pair[block(tap * 4 + 2 - 2 * core + j), 128:256] = got_b[tap, j]


def grad_second_kernel(
    place, g0, g1, g2, g3, weight, got_a, got_b, after, own, give, pair, wide
):
    y = place[0]
    temporal_pair(place, weight, got_a, got_b, pair)
    for d, piece in enumerate((g0, g1, g2, g3)):
        yb = lax.rem(y - d + 4, 4)
        frames(piece[...], wide, lambda s: block((1 - s) * 4 + yb))

    def step(i, carry):
        rows = pl.ds(pl.multiple_of(i * 256, 256), 256)
        total = jnp.zeros((256, 256), F32)
        for k in range(3):
            total += lax.dot_general(
                wide[rows, k * 512 : k * 512 + 512], pair[k], NT, preferred_element_type=F32
            )
        own[rows, :] = total[:, :128]
        give[rows, :] = total[:, 128:].astype(BF)
        return carry

    lax.fori_loop(0, 4, step, 0)


def spatial_out_kernel(place, h0, h1, h2, h3, pair, own, give, wide):
    y = place[0]
    for d, piece in enumerate((h0, h1, h2, h3)):
        yb = lax.rem(y - d + 4, 4)
        unfold(piece[...], wide, lambda sa, sb: block(((sa + 1) * 3 + sb + 1) * 4 + yb))

    def step(i, carry):
        rows = pl.ds(pl.multiple_of(i * 256, 256), 256)
        left = wide[pl.ds(2 * i, 2)].reshape(256, 4608)
        total = jnp.dot(left, pair[...], preferred_element_type=F32)
        own[rows, :] = total[:, :128]
        give[rows, :] = total[:, 128:].astype(BF)
        return carry

    lax.fori_loop(0, 4, step, 0)


def both_back_kernel(
    place, b0, b1, spatial, temporal, got_a, got_b, after,
    own_back, own_ahead, o1, o2, o3, pair, wide, pair_t, wide_t, total
):
    y = place[0]
    for tap in range(9):
        pair[:, tap * 256 : tap * 256 + 256] = spatial[tap * 512 : tap * 512 + 512, :]
    fill_grads((b0, b1), wide, (1, 0, -1))
    temporal_pair(place, temporal, got_a, got_b, pair_t)
    for j, piece in enumerate((b0, b1)):
        frames(piece[1], wide_t, lambda s: slice((s + 1) * 256 + j * 128, (s + 1) * 256 + j * 128 + 128))

    def spread(rows, own, part):
        own[rows, :] = total[:, block(y)]
        for d, out in enumerate((o1, o2, o3)):
            out[part, rows, :] = total[:, block(lax.rem(y + d + 1, 4))].astype(BF)

    def step(i, carry):
        rows = pl.ds(pl.multiple_of(i * 256, 256), 256)
        left = wide[pl.ds(2 * i, 2)].reshape(256, 2304)
        total[...] = lax.dot_general(left, pair[...], NT, preferred_element_type=F32)
        spread(rows, own_back, 0)
        total[...] = jnp.dot(
            wide_t[rows, :], pair_t[...].reshape(768, 512), preferred_element_type=F32
        )
        spread(rows, own_ahead, 1)
        return carry

    lax.fori_loop(0, 4, step, 0)


def fill_grads(pieces, wide, steps):
    for j, piece in enumerate(pieces):

        def column(sa, sb):
            at = (steps.index(sa) * 3 + 1 - sb) * 256 + j * 128
            return slice(at, at + 128)

        unfold(piece[0], wide, column, steps)


def transposed(y, pieces, target):
    for d, piece in enumerate(pieces):
        target[block(lax.rem(y - d + 4, 4)), :] = piece[...].T


def place_tap(place, total, keep, give, tap):
    x_hi, core, x_lo = place[1], place[2], place[3]
    for xr in range(2):
        for z in range(8):
            z2, z1, z0 = z // 4, z // 2 % 2, z % 2
            row = (lax.rem(x_lo + xr, 2) * 2 + z2) * 128 + z0 * 64
            col = block(lax.rem(x_hi + z1, 2))
            mine = pl.ds(pl.multiple_of(row + core * 32, 32), 32)
            other = pl.ds(pl.multiple_of(row + 32 - core * 32, 32), 32)
            keep[xr, z, tap] = total[mine, col]
            give[xr, z, tap] = total[other, col].astype(BF)


def spatial_taps(place, first, wide, keep, give, total, taps):
    def step(tap, carry):
        cols = pl.ds(pl.multiple_of(tap * 256, 256), 256)
        total[...] = jnp.dot(
            first[...], wide[:, :, cols].reshape(ROWS, 256), preferred_element_type=F32
        )
        place_tap(place, total, keep, give, tap)
        return carry

    lax.fori_loop(0, taps, step, 0)


def early_grads_kernel(place, h0, h1, h2, h3, b0, b1, keep, give, first, wide, total):
    transposed(place[0], (h0, h1, h2, h3), first)
    fill_grads((b0, b1), wide, (1, 0))
    spatial_taps(place, first, wide, keep, give, total, 6)


def late_grads_kernel(
    place, h0, h1, h2, h3, g0, g1, g2, g3, b0, b1, after, keep, give, first, grads, wide, tall, total
):
    transposed(place[0], (h0, h1, h2, h3), first)
    transposed(place[0], (g0, g1, g2, g3), grads)
    fill_grads((b0, b1), wide, (-1,))
    for j, piece in enumerate((b0, b1)):
        frames(piece[1], tall, lambda s: slice((s + 1) * 256 + j * 128, (s + 1) * 256 + j * 128 + 128))
    spatial_taps(place, first, wide, keep, give, total, 3)

    def step(tap, carry):
        cols = pl.ds(pl.multiple_of(tap * 256, 256), 256)
        total[...] = jnp.dot(grads[...], tall[:, cols], preferred_element_type=F32)
        place_tap(place, total, keep, give, tap + 3)
        return carry

    lax.fori_loop(0, 3, step, 0)


def core_sum(keep, give):
    got = data_move(give, 1).astype(F32)
    return keep[0] + got[0], (keep[1] + got[1]).astype(BF)


def x_lo_sum(keep, give):
    return (keep + data_move(give, 16).astype(F32)).astype(BF)


def per_device(clips, out_grad, spatial_weight, temporal_weight):
    tensor, data = lax.axis_index("tensor"), lax.axis_index("dp")
    x_hi, core = tensor % 2, data % 2
    z_mid = (data // 4) % 2
    place = jnp.stack([tensor // 2, x_hi, core, data // 16]).astype(jnp.int32)
    grad_scale = 1.0 / jnp.sqrt(jnp.float32(32768))
    clip_rows = clips.reshape(ROWS, 128)
    grads = out_grad.reshape(ROWS, 128)
    spatial = spatial_weight.reshape(9, 1024, 128)
    temporal = temporal_weight
    piece, wide_piece = shape((ROWS, 128), BF), shape((ROWS, 128), F32)

    cross = [
        (d * 8 + t, ((d + 16) % 32) * 8 + (t ^ 1)) for d in range(32) for t in range(8)
    ]
    (spatial_give,) = call(
        spatial_give_kernel, [shape((9, 2, 128, 128), BF)], [], [place, spatial], 0, "spatial_give"
    )
    (hidden_first,) = call(
        first_act_kernel, [piece], [], [clip_rows, spatial_give], 10**6, "first_act", unread=1
    )
    spatial_a = lax.ppermute(spatial_give, ("dp", "tensor"), cross)
    first_all = [hidden_first] + [tensor_move(hidden_first, d, 0) for d in (1, 2, 3)]
    (temporal_give,) = call(
        temporal_give_kernel,
        [shape((3, 2, 128, 128), BF)],
        [],
        [place, temporal, hidden_first],
        10**6,
        "temporal_give",
        unread=1,
    )
    spatial_a, temporal_give, grads, first_all = lax.optimization_barrier(
        (spatial_a, temporal_give, grads, first_all)
    )
    spatial_b = data_move(spatial_a, 1)
    grads_all = [grads] + [tensor_move(grads, d, 0) for d in (1, 2, 3)]
    temporal_a = lax.ppermute(temporal_give, ("dp", "tensor"), cross)
    temporal_b = data_move(temporal_a, 1)
    temporal_args = [temporal, temporal_a, temporal_b]
    (spatial_pair,) = call(
        spatial_pair_kernel,
        [shape((4608, 256), BF)],
        [],
        [place, spatial, spatial_a, spatial_b],
        10**6,
        "spatial_pair",
    )
    out_own, out_give = call(
        spatial_out_kernel,
        [wide_piece, piece],
        [pltpu.VMEM((8, 128, 4608), BF)],
        [place] + first_all + [spatial_pair],
        2 * ROWS * 4608 * 256,
        "spatial_out",
    )
    out_got = tensor_move(out_give, 0, 1)
    second_own, second_give = call(
        grad_second_kernel,
        [wide_piece, piece],
        [pltpu.VMEM((3, 256, 512), BF), pltpu.VMEM((ROWS, 1536), BF)],
        [place] + grads_all + temporal_args + [out_give],
        2 * ROWS * 1536 * 256,
        "grad_second",
        unread=1,
    )
    second_got = tensor_move(second_give, 0, 1)
    (both,) = call(
        second_act_kernel,
        [shape((2, ROWS, 128), BF)],
        [],
        [out_own, out_got, second_own, second_got],
        10**7,
        "second_act",
    )
    both_pair = [both, tensor_move(both, 0, 1)]

    half = [shape((2, 8, 6, 32, 128), F32), shape((2, 8, 6, 32, 128), BF)]
    keep, give = call(
        early_grads_kernel,
        half,
        [
            pltpu.VMEM((512, ROWS), BF),
            pltpu.VMEM((8, 128, 1536), BF),
            pltpu.VMEM((512, 256), F32),
        ],
        [place] + first_all + both_pair,
        2 * ROWS * 1536 * 512,
        "early_grads",
    )
    late_keep, late_give = call(
        late_grads_kernel,
        half,
        [
            pltpu.VMEM((512, ROWS), BF),
            pltpu.VMEM((512, ROWS), BF),
            pltpu.VMEM((8, 128, 768), BF),
            pltpu.VMEM((ROWS, 768), BF),
            pltpu.VMEM((512, 256), F32),
        ],
        [place] + first_all + grads_all + both_pair + [give],
        2 * ROWS * 1536 * 512,
        "late_grads",
        unread=1,
    )
    early_local = x_lo_sum(*core_sum(keep, give))
    own_back, own_ahead, *parts = call(
        both_back_kernel,
        [wide_piece, wide_piece] + [shape((2, ROWS, 128), BF)] * 3,
        [
            pltpu.VMEM((512, 2304), BF),
            pltpu.VMEM((8, 128, 2304), BF),
            pltpu.VMEM((3, 256, 512), BF),
            pltpu.VMEM((ROWS, 768), BF),
            pltpu.VMEM((256, 512), F32),
        ],
        [place] + both_pair + [spatial_pair] + temporal_args + [late_give],
        2 * ROWS * 3072 * 512,
        "both_back",
        unread=1,
    )

    late_local = x_lo_sum(*core_sum(late_keep, late_give))
    local = jnp.concatenate([early_local, late_local], axis=1)
    local, parts = lax.optimization_barrier((local, parts))
    parts = [tensor_move(parts[d - 1], d, 0) for d in (1, 2, 3)]
    local = lax.all_to_all(
        local,
        "dp",
        split_axis=0,
        concat_axis=0,
        tiled=True,
        axis_index_groups=Z_GROUPS,
    )
    share = (jnp.sum(local.astype(F32), axis=0) * grad_scale).astype(BF)
    move = []
    for d in range(32):
        for t in range(8):
            if (d // 4) % 2 != t % 2:
                move.append((d * 8 + t, (d ^ 4) * 8 + (t ^ 1)))
    moved = lax.ppermute(share, ("dp", "tensor"), move)
    share = jnp.where(z_mid == x_hi, share, moved)
    spatial_share = share[:9].reshape(3, 3, 32, 128)
    temporal_share = share[9:].swapaxes(1, 2)

    mixed, clip_grad = call(
        finish_kernel,
        [piece, piece],
        [],
        [clip_rows, grads, own_back, own_ahead] + parts,
        10**7,
        "finish",
    )
    return (
        mixed.reshape(clips.shape),
        clip_grad.reshape(clips.shape),
        spatial_share,
        temporal_share,
    )


def solution(mesh):
    placed = (
        P("dp", None, None, None, "tensor"),
        P("dp", None, None, None, "tensor"),
        P(None, None, None, "tensor"),
        P(None, "tensor", None),
    )
    return jax.shard_map(
        per_device,
        mesh=mesh,
        in_specs=placed,
        out_specs=(
            P("dp", None, None, None, "tensor"),
            P("dp", None, None, None, "tensor"),
            P(None, None, "dp", "tensor"),
            P(None, "tensor", "dp"),
        ),
        check_vma=False,
    )
```

```python
import jax
import jax.numpy as jnp
from jax import lax
from jax.experimental import pallas as pl
from jax.experimental.pallas import tpu as pltpu
from jax.sharding import PartitionSpec as P

GS = 32
ROWS = 1024
BF = jnp.bfloat16
F32 = jnp.float32
NT = (((1,), (1,)), ((), ()))
Z_GROUPS = [[l * 16 + z * 2 + c for z in range(8)] for l in range(2) for c in range(2)]


def tensor_move(values, y_step, x_flip):
    pairs = [(t, ((t // 2 + y_step) % 4) * 2 + (t % 2 ^ x_flip)) for t in range(8)]
    return lax.ppermute(values, "tensor", pairs)


def data_move(values, bits):
    return lax.ppermute(values, "dp", [(d, d ^ bits) for d in range(32)])


def block(index):
    return pl.ds(pl.multiple_of(index * 128, 128), 128)


def call(body, outs, scratch, args, flops, name, unread=0):
    total = sum(a.size * a.dtype.itemsize for a in args)
    total += sum(o.size * o.dtype.itemsize for o in outs)
    smem = pl.BlockSpec(memory_space=pltpu.SMEM)
    vmem = pl.BlockSpec(memory_space=pltpu.VMEM)
    specs = [smem if a.dtype == jnp.int32 else vmem for a in args]
    if unread:
        specs[-unread:] = [pl.BlockSpec(memory_space=pl.ANY)] * unread
    result = pl.pallas_call(
        body,
        out_shape=outs,
        in_specs=specs,
        out_specs=[vmem] * len(outs),
        scratch_shapes=scratch,
        compiler_params=pltpu.CompilerParams(vmem_limit_bytes=48 * 1024 * 1024),
        cost_estimate=pl.CostEstimate(flops=flops, bytes_accessed=total, transcendentals=0),
        name=name,
    )(*args)
    return list(result)


def shape(dims, dtype):
    return jax.ShapeDtypeStruct(dims, dtype)


def group_mean(values):
    sums = jnp.sum(values, axis=0, keepdims=True)
    rows = lax.broadcasted_iota(jnp.int32, (128, 128), 0) // GS
    lanes = lax.broadcasted_iota(jnp.int32, (128, 128), 1) // GS
    same = (rows == lanes).astype(F32)
    sums = jnp.broadcast_to(sums, (8, 128))
    sums = jnp.dot(sums, same, precision=lax.Precision.HIGHEST, preferred_element_type=F32)
    return sums[0:1] * (1.0 / (ROWS * GS))


def normalize(values):
    offsets = values - group_mean(values)
    scale = lax.rsqrt(group_mean(offsets * offsets) + 1e-05)
    return offsets * scale, scale


def gate_of(unit):
    return 1.0 / (1.0 + jnp.exp(-unit))


def act_back(unit, scale, gate, grads):
    inner = grads * (gate * (1.0 + unit * (1.0 - gate)))
    return scale * (inner - group_mean(inner) - unit * group_mean(inner * unit))


def first_act_kernel(clips, after, hidden):
    unit, _ = normalize(clips[...].astype(F32))
    hidden[...] = (unit * gate_of(unit)).astype(BF)


def second_act_kernel(out_own, out_got, grad_own, grad_got, both):
    unit, scale = normalize(out_own[...] + out_got[...].astype(F32))
    gate = gate_of(unit)
    both[1] = (unit * gate).astype(BF)
    received = grad_own[...] + grad_got[...].astype(F32)
    both[0] = act_back(unit, scale, gate, received).astype(BF)


def finish_kernel(clips, out_grad, own_back, own_ahead, got_a, got_b, got_c, mixed, clip_grad):
    rows = clips[...].astype(F32)
    ahead = own_ahead[...] + got_a[1].astype(F32) + got_b[1].astype(F32) + got_c[1].astype(F32)
    mixed[...] = (rows + ahead).astype(BF)
    unit, scale = normalize(rows)
    grads = own_back[...] + got_a[0].astype(F32) + got_b[0].astype(F32) + got_c[0].astype(F32)
    back = act_back(unit, scale, gate_of(unit), grads)
    clip_grad[...] = (out_grad[...].astype(F32) + back).astype(BF)


def unfold(values, target, column, steps=(-1, 0, 1)):
    wide = values.astype(F32)
    place = lax.broadcasted_iota(jnp.int32, (ROWS, 128), 0) % 16
    for sb in (-1, 0, 1):
        moved = wide
        if sb:
            moved = pltpu.roll(wide, (-sb) % ROWS, 0)
            moved = jnp.where(place == (15 if sb == 1 else 0), 0.0, moved)
        moved = moved.astype(BF).reshape(8, 128, 128)
        zeros = jnp.zeros((8, 16, 128), BF)
        for sa in steps:
            at = column(sa, sb)
            if sa == 0:
                target[:, :, at] = moved
            elif sa == 1:
                target[:, 0:112, at] = moved[:, 16:]
                target[:, 112:128, at] = zeros
            else:
                target[:, 16:128, at] = moved[:, :112]
                target[:, 0:16, at] = zeros


def frames(values, target, column):
    zeros = jnp.zeros((128, 128), BF)
    for s in (-1, 0, 1):
        at = column(s)
        if s == 0:
            target[:, at] = values
        elif s == 1:
            target[0:896, at] = values[128:]
            target[896:1024, at] = zeros
        else:
            target[128:1024, at] = values[:896]
            target[0:128, at] = zeros


def temporal_pair(place, weight, got_a, got_b, pair):
    x_hi, core = place[1], place[2]
    for k in range(3):
        for yb in range(4):
            pair[k, 0:128, yb * 128 : yb * 128 + 128] = weight[k, :, block(2 * yb + x_hi)]
        for j in range(2):
            pair[k, 128:256, block(2 * core + j)] = got_a[k, j]
            pair[k, 128:256, block(2 - 2 * core + j)] = got_b[k, j]


def spatial_give_kernel(place, weight, give):
    x_hi, core = place[1], place[2]
    for j in range(2):
        at = block(2 * (2 * core + j) + 1 - x_hi)
        for tap in range(9):
            give[tap, j] = weight[tap, at, :]


def temporal_give_kernel(place, weight, after, give):
    x_hi, core = place[1], place[2]
    for j in range(2):
        at = block(2 * (2 * core + j) + 1 - x_hi)
        for k in range(3):
            give[k, j] = weight[k, :, at]


def spatial_pair_kernel(place, weight, got_a, got_b, after, pair):
    x_hi, core = place[1], place[2]
    for tap in range(9):
        for yb in range(4):
            at = tap * 512 + yb * 128
            pair[at : at + 128, 0:128] = weight[tap, block(2 * yb + x_hi), :]
        for j in range(2):
            pair[block(tap * 4 + 2 * core + j), 128:256] = got_a[tap, j]
            pair[block(tap * 4 + 2 - 2 * core + j), 128:256] = got_b[tap, j]


def grad_second_kernel(
    place, g0, g1, g2, g3, weight, got_a, got_b, after, own, give, pair, wide
):
    y = place[0]
    temporal_pair(place, weight, got_a, got_b, pair)
    for d, piece in enumerate((g0, g1, g2, g3)):
        yb = lax.rem(y - d + 4, 4)
        frames(piece[...], wide, lambda s: block((1 - s) * 4 + yb))

    def step(i, carry):
        rows = pl.ds(pl.multiple_of(i * 256, 256), 256)
        total = jnp.zeros((256, 256), F32)
        for k in range(3):
            total += lax.dot_general(
                wide[rows, k * 512 : k * 512 + 512], pair[k], NT, preferred_element_type=F32
            )
        own[rows, :] = total[:, :128]
        give[rows, :] = total[:, 128:].astype(BF)
        return carry

    lax.fori_loop(0, 4, step, 0)


def spatial_product(y, pieces, half, wide, result):
    for d, piece in enumerate(pieces):
        yb = lax.rem(y - d + 4, 4)
        unfold(piece[...], wide, lambda sa, sb: block(((sa + 1) * 3 + sb + 1) * 4 + yb))

    def step(i, carry):
        rows = pl.ds(pl.multiple_of(i * 256, 256), 256)
        left = wide[pl.ds(2 * i, 2)].reshape(256, 4608)
        result[rows, :] = jnp.dot(left, half[...], preferred_element_type=F32).astype(result.dtype)
        return carry

    lax.fori_loop(0, 4, step, 0)


def spatial_partner_kernel(place, h0, h1, h2, h3, got_a, got_b, give, half, wide):
    core = place[2]
    for tap in range(9):
        for j in range(2):
            half[block(tap * 4 + 2 * core + j), :] = got_a[tap, j]
            half[block(tap * 4 + 2 - 2 * core + j), :] = got_b[tap, j]
    spatial_product(place[0], (h0, h1, h2, h3), half, wide, give)


def spatial_own_kernel(place, h0, h1, h2, h3, weight, after, own, half, wide):
    x_hi = place[1]
    for tap in range(9):
        for yb in range(4):
            at = tap * 512 + yb * 128
            half[at : at + 128, :] = weight[tap, block(2 * yb + x_hi), :]
    spatial_product(place[0], (h0, h1, h2, h3), half, wide, own)


def both_back_kernel(
    place, b0, b1, spatial, temporal, got_a, got_b, after,
    own_back, own_ahead, o1, o2, o3, pair, wide, pair_t, wide_t, total
):
    y = place[0]
    for tap in range(9):
        pair[:, tap * 256 : tap * 256 + 256] = spatial[tap * 512 : tap * 512 + 512, :]
    fill_grads((b0, b1), wide, (1, 0, -1))
    temporal_pair(place, temporal, got_a, got_b, pair_t)
    for j, piece in enumerate((b0, b1)):
        frames(piece[1], wide_t, lambda s: slice((s + 1) * 256 + j * 128, (s + 1) * 256 + j * 128 + 128))

    def spread(rows, own, part):
        own[rows, :] = total[:, block(y)]
        for d, out in enumerate((o1, o2, o3)):
            out[part, rows, :] = total[:, block(lax.rem(y + d + 1, 4))].astype(BF)

    def step(i, carry):
        rows = pl.ds(pl.multiple_of(i * 256, 256), 256)
        left = wide[pl.ds(2 * i, 2)].reshape(256, 2304)
        total[...] = lax.dot_general(left, pair[...], NT, preferred_element_type=F32)
        spread(rows, own_back, 0)
        total[...] = jnp.dot(
            wide_t[rows, :], pair_t[...].reshape(768, 512), preferred_element_type=F32
        )
        spread(rows, own_ahead, 1)
        return carry

    lax.fori_loop(0, 4, step, 0)


def fill_grads(pieces, wide, steps):
    for j, piece in enumerate(pieces):

        def column(sa, sb):
            at = (steps.index(sa) * 3 + 1 - sb) * 256 + j * 128
            return slice(at, at + 128)

        unfold(piece[0], wide, column, steps)


def transposed(y, pieces, target):
    for d, piece in enumerate(pieces):
        target[block(lax.rem(y - d + 4, 4)), :] = piece[...].T


def place_tap(place, total, keep, give, tap):
    x_hi, core, x_lo = place[1], place[2], place[3]
    for xr in range(2):
        for z in range(8):
            z2, z1, z0 = z // 4, z // 2 % 2, z % 2
            row = (lax.rem(x_lo + xr, 2) * 2 + z2) * 128 + z0 * 64
            col = block(lax.rem(x_hi + z1, 2))
            mine = pl.ds(pl.multiple_of(row + core * 32, 32), 32)
            other = pl.ds(pl.multiple_of(row + 32 - core * 32, 32), 32)
            keep[xr, z, tap] = total[mine, col]
            give[xr, z, tap] = total[other, col].astype(BF)


def spatial_taps(place, first, wide, keep, give, total, taps):
    def step(tap, carry):
        cols = pl.ds(pl.multiple_of(tap * 256, 256), 256)
        total[...] = jnp.dot(
            first[...], wide[:, :, cols].reshape(ROWS, 256), preferred_element_type=F32
        )
        place_tap(place, total, keep, give, tap)
        return carry

    lax.fori_loop(0, taps, step, 0)


def early_grads_kernel(place, h0, h1, h2, h3, b0, b1, after, keep, give, first, wide, total):
    transposed(place[0], (h0, h1, h2, h3), first)
    fill_grads((b0, b1), wide, (1, 0))
    spatial_taps(place, first, wide, keep, give, total, 6)


def late_grads_kernel(
    place, h0, h1, h2, h3, g0, g1, g2, g3, b0, b1, after, keep, give, first, grads, wide, tall, total
):
    transposed(place[0], (h0, h1, h2, h3), first)
    transposed(place[0], (g0, g1, g2, g3), grads)
    fill_grads((b0, b1), wide, (-1,))
    for j, piece in enumerate((b0, b1)):
        frames(piece[1], tall, lambda s: slice((s + 1) * 256 + j * 128, (s + 1) * 256 + j * 128 + 128))
    spatial_taps(place, first, wide, keep, give, total, 3)

    def step(tap, carry):
        cols = pl.ds(pl.multiple_of(tap * 256, 256), 256)
        total[...] = jnp.dot(grads[...], tall[:, cols], preferred_element_type=F32)
        place_tap(place, total, keep, give, tap + 3)
        return carry

    lax.fori_loop(0, 3, step, 0)


def core_sum(keep, give):
    got = data_move(give, 1).astype(F32)
    return keep[0] + got[0], (keep[1] + got[1]).astype(BF)


def x_lo_sum(keep, give):
    return (keep + data_move(give, 16).astype(F32)).astype(BF)


def per_device(clips, out_grad, spatial_weight, temporal_weight):
    tensor, data = lax.axis_index("tensor"), lax.axis_index("dp")
    x_hi, core = tensor % 2, data % 2
    z_mid = (data // 4) % 2
    place = jnp.stack([tensor // 2, x_hi, core, data // 16]).astype(jnp.int32)
    grad_scale = 1.0 / jnp.sqrt(jnp.float32(32768))
    clip_rows = clips.reshape(ROWS, 128)
    grads = out_grad.reshape(ROWS, 128)
    spatial = spatial_weight.reshape(9, 1024, 128)
    temporal = temporal_weight
    piece, wide_piece = shape((ROWS, 128), BF), shape((ROWS, 128), F32)

    cross = [
        (d * 8 + t, ((d + 16) % 32) * 8 + (t ^ 1)) for d in range(32) for t in range(8)
    ]
    (spatial_give,) = call(
        spatial_give_kernel, [shape((9, 2, 128, 128), BF)], [], [place, spatial], 0, "spatial_give"
    )
    (hidden_first,) = call(
        first_act_kernel, [piece], [], [clip_rows, spatial_give], 10**6, "first_act", unread=1
    )
    spatial_a = lax.ppermute(spatial_give, ("dp", "tensor"), cross)
    first_all = [hidden_first] + [tensor_move(hidden_first, d, 0) for d in (1, 2, 3)]
    (temporal_give,) = call(
        temporal_give_kernel,
        [shape((3, 2, 128, 128), BF)],
        [],
        [place, temporal, hidden_first],
        10**6,
        "temporal_give",
        unread=1,
    )
    spatial_a, temporal_give, grads, first_all = lax.optimization_barrier(
        (spatial_a, temporal_give, grads, first_all)
    )
    spatial_b = data_move(spatial_a, 1)
    grads_all = [grads] + [tensor_move(grads, d, 0) for d in (1, 2, 3)]
    temporal_a = lax.ppermute(temporal_give, ("dp", "tensor"), cross)
    out_scratch = [pltpu.VMEM((4608, 128), BF), pltpu.VMEM((8, 128, 4608), BF)]
    (out_give,) = call(
        spatial_partner_kernel,
        [piece],
        out_scratch,
        [place] + first_all + [spatial_a, spatial_b],
        ROWS * 4608 * 256,
        "spatial_partner",
    )
    temporal_a, out_give = lax.optimization_barrier((temporal_a, out_give))
    temporal_b = data_move(temporal_a, 1)
    temporal_args = [temporal, temporal_a, temporal_b]
    (out_own,) = call(
        spatial_own_kernel,
        [wide_piece],
        out_scratch,
        [place] + first_all + [spatial, out_give],
        ROWS * 4608 * 256,
        "spatial_own",
        unread=1,
    )
    out_got = tensor_move(out_give, 0, 1)
    (spatial_pair,) = call(
        spatial_pair_kernel,
        [shape((4608, 256), BF)],
        [],
        [place, spatial, spatial_a, spatial_b, out_give],
        10**6,
        "spatial_pair",
        unread=1,
    )
    second_own, second_give = call(
        grad_second_kernel,
        [wide_piece, piece],
        [pltpu.VMEM((3, 256, 512), BF), pltpu.VMEM((ROWS, 1536), BF)],
        [place] + grads_all + temporal_args + [out_give],
        2 * ROWS * 1536 * 256,
        "grad_second",
        unread=1,
    )
    second_got = tensor_move(second_give, 0, 1)
    (both,) = call(
        second_act_kernel,
        [shape((2, ROWS, 128), BF)],
        [],
        [out_own, out_got, second_own, second_got],
        10**7,
        "second_act",
    )
    both_pair = [both, tensor_move(both, 0, 1)]

    half = [shape((2, 8, 6, 32, 128), F32), shape((2, 8, 6, 32, 128), BF)]
    keep, give = call(
        early_grads_kernel,
        half,
        [
            pltpu.VMEM((512, ROWS), BF),
            pltpu.VMEM((8, 128, 1536), BF),
            pltpu.VMEM((512, 256), F32),
        ],
        [place] + first_all + both_pair + [spatial_pair],
        2 * ROWS * 1536 * 512,
        "early_grads",
        unread=1,
    )
    late_keep, late_give = call(
        late_grads_kernel,
        half,
        [
            pltpu.VMEM((512, ROWS), BF),
            pltpu.VMEM((512, ROWS), BF),
            pltpu.VMEM((8, 128, 768), BF),
            pltpu.VMEM((ROWS, 768), BF),
            pltpu.VMEM((512, 256), F32),
        ],
        [place] + first_all + grads_all + both_pair + [give],
        2 * ROWS * 1536 * 512,
        "late_grads",
        unread=1,
    )
    early_local = x_lo_sum(*core_sum(keep, give))
    own_back, own_ahead, *parts = call(
        both_back_kernel,
        [wide_piece, wide_piece] + [shape((2, ROWS, 128), BF)] * 3,
        [
            pltpu.VMEM((512, 2304), BF),
            pltpu.VMEM((8, 128, 2304), BF),
            pltpu.VMEM((3, 256, 512), BF),
            pltpu.VMEM((ROWS, 768), BF),
            pltpu.VMEM((256, 512), F32),
        ],
        [place] + both_pair + [spatial_pair] + temporal_args + [late_give],
        2 * ROWS * 3072 * 512,
        "both_back",
        unread=1,
    )

    late_local = x_lo_sum(*core_sum(late_keep, late_give))
    local = jnp.concatenate([early_local, late_local], axis=1)
    local, parts = lax.optimization_barrier((local, parts))
    parts = [tensor_move(parts[d - 1], d, 0) for d in (1, 2, 3)]
    local = lax.all_to_all(
        local,
        "dp",
        split_axis=0,
        concat_axis=0,
        tiled=True,
        axis_index_groups=Z_GROUPS,
    )
    share = (jnp.sum(local.astype(F32), axis=0) * grad_scale).astype(BF)
    move = []
    for d in range(32):
        for t in range(8):
            if (d // 4) % 2 != t % 2:
                move.append((d * 8 + t, (d ^ 4) * 8 + (t ^ 1)))
    moved = lax.ppermute(share, ("dp", "tensor"), move)
    share = jnp.where(z_mid == x_hi, share, moved)
    spatial_share = share[:9].reshape(3, 3, 32, 128)
    temporal_share = share[9:].swapaxes(1, 2)

    mixed, clip_grad = call(
        finish_kernel,
        [piece, piece],
        [],
        [clip_rows, grads, own_back, own_ahead] + parts,
        10**7,
        "finish",
    )
    return (
        mixed.reshape(clips.shape),
        clip_grad.reshape(clips.shape),
        spatial_share,
        temporal_share,
    )


def solution(mesh):
    placed = (
        P("dp", None, None, None, "tensor"),
        P("dp", None, None, None, "tensor"),
        P(None, None, None, "tensor"),
        P(None, "tensor", None),
    )
    return jax.shard_map(
        per_device,
        mesh=mesh,
        in_specs=placed,
        out_specs=(
            P("dp", None, None, None, "tensor"),
            P("dp", None, None, None, "tensor"),
            P(None, None, "dp", "tensor"),
            P(None, "tensor", "dp"),
        ),
        check_vma=False,
    )
```

```python
import jax
import jax.numpy as jnp
from jax import lax
from jax.experimental import pallas as pl
from jax.experimental.pallas import tpu as pltpu
from jax.sharding import PartitionSpec as P

GS = 32
ROWS = 1024
BF = jnp.bfloat16
F32 = jnp.float32
NT = (((1,), (1,)), ((), ()))
Z_GROUPS = [[l * 16 + z * 2 + c for z in range(8)] for l in range(2) for c in range(2)]


def tensor_move(values, y_step, x_flip):
    pairs = [(t, ((t // 2 + y_step) % 4) * 2 + (t % 2 ^ x_flip)) for t in range(8)]
    return lax.ppermute(values, "tensor", pairs)


def data_move(values, bits):
    return lax.ppermute(values, "dp", [(d, d ^ bits) for d in range(32)])


def block(index):
    return pl.ds(pl.multiple_of(index * 128, 128), 128)


def call(body, outs, scratch, args, flops, name, unread=0):
    total = sum(a.size * a.dtype.itemsize for a in args)
    total += sum(o.size * o.dtype.itemsize for o in outs)
    smem = pl.BlockSpec(memory_space=pltpu.SMEM)
    vmem = pl.BlockSpec(memory_space=pltpu.VMEM)
    specs = [smem if a.dtype == jnp.int32 else vmem for a in args]
    if unread:
        specs[-unread:] = [pl.BlockSpec(memory_space=pl.ANY)] * unread
    result = pl.pallas_call(
        body,
        out_shape=outs,
        in_specs=specs,
        out_specs=[vmem] * len(outs),
        scratch_shapes=scratch,
        compiler_params=pltpu.CompilerParams(vmem_limit_bytes=48 * 1024 * 1024),
        cost_estimate=pl.CostEstimate(flops=flops, bytes_accessed=total, transcendentals=0),
        name=name,
    )(*args)
    return list(result)


def shape(dims, dtype):
    return jax.ShapeDtypeStruct(dims, dtype)


def group_mean(values):
    sums = jnp.sum(values, axis=0, keepdims=True)
    rows = lax.broadcasted_iota(jnp.int32, (128, 128), 0) // GS
    lanes = lax.broadcasted_iota(jnp.int32, (128, 128), 1) // GS
    same = (rows == lanes).astype(F32)
    sums = jnp.broadcast_to(sums, (8, 128))
    sums = jnp.dot(sums, same, precision=lax.Precision.HIGHEST, preferred_element_type=F32)
    return sums[0:1] * (1.0 / (ROWS * GS))


def normalize(values):
    offsets = values - group_mean(values)
    scale = lax.rsqrt(group_mean(offsets * offsets) + 1e-05)
    return offsets * scale, scale


def gate_of(unit):
    return 1.0 / (1.0 + jnp.exp(-unit))


def act_back(unit, scale, gate, grads):
    inner = grads * (gate * (1.0 + unit * (1.0 - gate)))
    return scale * (inner - group_mean(inner) - unit * group_mean(inner * unit))


def first_act_kernel(clips, after, hidden):
    unit, _ = normalize(clips[...].astype(F32))
    hidden[...] = (unit * gate_of(unit)).astype(BF)


def second_act_kernel(out_own, out_got, grad_own, grad_got, both):
    unit, scale = normalize(out_own[...] + out_got[...].astype(F32))
    gate = gate_of(unit)
    both[1] = (unit * gate).astype(BF)
    received = grad_own[...] + grad_got[...].astype(F32)
    both[0] = act_back(unit, scale, gate, received).astype(BF)


def finish_kernel(clips, out_grad, own_back, own_ahead, got_a, got_b, got_c, mixed, clip_grad):
    rows = clips[...].astype(F32)
    ahead = own_ahead[...] + got_a[1].astype(F32) + got_b[1].astype(F32) + got_c[1].astype(F32)
    mixed[...] = (rows + ahead).astype(BF)
    unit, scale = normalize(rows)
    grads = own_back[...] + got_a[0].astype(F32) + got_b[0].astype(F32) + got_c[0].astype(F32)
    back = act_back(unit, scale, gate_of(unit), grads)
    clip_grad[...] = (out_grad[...].astype(F32) + back).astype(BF)


def unfold(values, target, column, steps=(-1, 0, 1)):
    wide = values.astype(F32)
    place = lax.broadcasted_iota(jnp.int32, (ROWS, 128), 0) % 16
    for sb in (-1, 0, 1):
        moved = wide
        if sb:
            moved = pltpu.roll(wide, (-sb) % ROWS, 0)
            moved = jnp.where(place == (15 if sb == 1 else 0), 0.0, moved)
        moved = moved.astype(BF).reshape(8, 128, 128)
        zeros = jnp.zeros((8, 16, 128), BF)
        for sa in steps:
            at = column(sa, sb)
            if sa == 0:
                target[:, :, at] = moved
            elif sa == 1:
                target[:, 0:112, at] = moved[:, 16:]
                target[:, 112:128, at] = zeros
            else:
                target[:, 16:128, at] = moved[:, :112]
                target[:, 0:16, at] = zeros


def frames(values, target, column):
    zeros = jnp.zeros((128, 128), BF)
    for s in (-1, 0, 1):
        at = column(s)
        if s == 0:
            target[:, at] = values
        elif s == 1:
            target[0:896, at] = values[128:]
            target[896:1024, at] = zeros
        else:
            target[128:1024, at] = values[:896]
            target[0:128, at] = zeros


def temporal_pair(place, weight, got_a, got_b, pair):
    x_hi, core = place[1], place[2]
    for k in range(3):
        for yb in range(4):
            pair[k, 0:128, yb * 128 : yb * 128 + 128] = weight[k, :, block(2 * yb + x_hi)]
        for j in range(2):
            pair[k, 128:256, block(2 * core + j)] = got_a[k, j]
            pair[k, 128:256, block(2 - 2 * core + j)] = got_b[k, j]


def spatial_give_kernel(place, weight, give):
    x_hi, core = place[1], place[2]
    for j in range(2):
        at = block(2 * (2 * core + j) + 1 - x_hi)
        for tap in range(9):
            give[tap, j] = weight[tap, at, :]


def temporal_give_kernel(place, weight, after, give):
    x_hi, core = place[1], place[2]
    for j in range(2):
        at = block(2 * (2 * core + j) + 1 - x_hi)
        for k in range(3):
            give[k, j] = weight[k, :, at]


def spatial_pair_kernel(place, weight, got_a, got_b, after, pair):
    x_hi, core = place[1], place[2]
    for tap in range(9):
        for yb in range(4):
            at = tap * 512 + yb * 128
            pair[at : at + 128, 0:128] = weight[tap, block(2 * yb + x_hi), :]
        for j in range(2):
            pair[block(tap * 4 + 2 * core + j), 128:256] = got_a[tap, j]
            pair[block(tap * 4 + 2 - 2 * core + j), 128:256] = got_b[tap, j]


def grad_second_kernel(
    place, g0, g1, g2, g3, weight, got_a, got_b, after, own, give, pair, wide
):
    y = place[0]
    temporal_pair(place, weight, got_a, got_b, pair)
    for d, piece in enumerate((g0, g1, g2, g3)):
        yb = lax.rem(y - d + 4, 4)
        frames(piece[...], wide, lambda s: block((1 - s) * 4 + yb))

    def step(i, carry):
        rows = pl.ds(pl.multiple_of(i * 256, 256), 256)
        total = jnp.zeros((256, 256), F32)
        for k in range(3):
            total += lax.dot_general(
                wide[rows, k * 512 : k * 512 + 512], pair[k], NT, preferred_element_type=F32
            )
        own[rows, :] = total[:, :128]
        give[rows, :] = total[:, 128:].astype(BF)
        return carry

    lax.fori_loop(0, 4, step, 0)


def spatial_product(y, pieces, half, wide, result):
    for d, piece in enumerate(pieces):
        yb = lax.rem(y - d + 4, 4)
        unfold(piece[...], wide, lambda sa, sb: block(((sa + 1) * 3 + sb + 1) * 4 + yb))

    def step(i, carry):
        rows = pl.ds(pl.multiple_of(i * 512, 512), 512)
        left = wide[pl.ds(4 * i, 4)].reshape(512, 4608)
        result[rows, :] = jnp.dot(left, half[...], preferred_element_type=F32).astype(result.dtype)
        return carry

    lax.fori_loop(0, 2, step, 0)


def spatial_partner_kernel(place, h0, h1, h2, h3, got_a, got_b, give, half, wide):
    core = place[2]
    for tap in range(9):
        for j in range(2):
            half[block(tap * 4 + 2 * core + j), :] = got_a[tap, j]
            half[block(tap * 4 + 2 - 2 * core + j), :] = got_b[tap, j]
    spatial_product(place[0], (h0, h1, h2, h3), half, wide, give)


def spatial_own_kernel(place, h0, h1, h2, h3, weight, after, own, half, wide):
    x_hi = place[1]
    for tap in range(9):
        for yb in range(4):
            at = tap * 512 + yb * 128
            half[at : at + 128, :] = weight[tap, block(2 * yb + x_hi), :]
    spatial_product(place[0], (h0, h1, h2, h3), half, wide, own)


def both_back_kernel(
    place, b0, b1, spatial, temporal, got_a, got_b, after,
    own_back, own_ahead, o1, o2, o3, pair, wide, pair_t, wide_t, total
):
    y = place[0]
    for tap in range(9):
        pair[:, tap * 256 : tap * 256 + 256] = spatial[tap * 512 : tap * 512 + 512, :]
    fill_grads((b0, b1), wide, (1, 0, -1))
    temporal_pair(place, temporal, got_a, got_b, pair_t)
    for j, piece in enumerate((b0, b1)):
        frames(piece[1], wide_t, lambda s: slice((s + 1) * 256 + j * 128, (s + 1) * 256 + j * 128 + 128))

    def spread(rows, own, part):
        own[rows, :] = total[:, block(y)]
        for d, out in enumerate((o1, o2, o3)):
            out[part, rows, :] = total[:, block(lax.rem(y + d + 1, 4))].astype(BF)

    def step(i, carry):
        rows = pl.ds(pl.multiple_of(i * 256, 256), 256)
        left = wide[pl.ds(2 * i, 2)].reshape(256, 2304)
        total[...] = lax.dot_general(left, pair[...], NT, preferred_element_type=F32)
        spread(rows, own_back, 0)
        total[...] = jnp.dot(
            wide_t[rows, :], pair_t[...].reshape(768, 512), preferred_element_type=F32
        )
        spread(rows, own_ahead, 1)
        return carry

    lax.fori_loop(0, 4, step, 0)


def fill_grads(pieces, wide, steps):
    for j, piece in enumerate(pieces):

        def column(sa, sb):
            at = (steps.index(sa) * 3 + 1 - sb) * 256 + j * 128
            return slice(at, at + 128)

        unfold(piece[0], wide, column, steps)


def transposed(y, pieces, target):
    for d, piece in enumerate(pieces):
        target[block(lax.rem(y - d + 4, 4)), :] = piece[...].T


def place_tap(place, total, keep, give, tap):
    x_hi, core, x_lo = place[1], place[2], place[3]
    for xr in range(2):
        for z in range(8):
            z2, z1, z0 = z // 4, z // 2 % 2, z % 2
            row = (lax.rem(x_lo + xr, 2) * 2 + z2) * 128 + z0 * 64
            col = block(lax.rem(x_hi + z1, 2))
            mine = pl.ds(pl.multiple_of(row + core * 32, 32), 32)
            other = pl.ds(pl.multiple_of(row + 32 - core * 32, 32), 32)
            keep[xr, z, tap] = total[mine, col]
            give[xr, z, tap] = total[other, col].astype(BF)


def spatial_taps(place, first, wide, keep, give, total, taps):
    def step(tap, carry):
        cols = pl.ds(pl.multiple_of(tap * 256, 256), 256)
        total[...] = jnp.dot(
            first[...], wide[:, :, cols].reshape(ROWS, 256), preferred_element_type=F32
        )
        place_tap(place, total, keep, give, tap)
        return carry

    lax.fori_loop(0, taps, step, 0)


def early_grads_kernel(place, h0, h1, h2, h3, b0, b1, after, keep, give, first, wide, total):
    transposed(place[0], (h0, h1, h2, h3), first)
    fill_grads((b0, b1), wide, (1, 0))
    spatial_taps(place, first, wide, keep, give, total, 6)


def late_grads_kernel(
    place, h0, h1, h2, h3, g0, g1, g2, g3, b0, b1, after, keep, give, first, grads, wide, tall, total
):
    transposed(place[0], (h0, h1, h2, h3), first)
    transposed(place[0], (g0, g1, g2, g3), grads)
    fill_grads((b0, b1), wide, (-1,))
    for j, piece in enumerate((b0, b1)):
        frames(piece[1], tall, lambda s: slice((s + 1) * 256 + j * 128, (s + 1) * 256 + j * 128 + 128))
    spatial_taps(place, first, wide, keep, give, total, 3)

    def step(tap, carry):
        cols = pl.ds(pl.multiple_of(tap * 256, 256), 256)
        total[...] = jnp.dot(grads[...], tall[:, cols], preferred_element_type=F32)
        place_tap(place, total, keep, give, tap + 3)
        return carry

    lax.fori_loop(0, 3, step, 0)


def core_sum(keep, give):
    got = data_move(give, 1).astype(F32)
    return keep[0] + got[0], (keep[1] + got[1]).astype(BF)


def x_lo_sum(keep, give):
    return (keep + data_move(give, 16).astype(F32)).astype(BF)


def per_device(clips, out_grad, spatial_weight, temporal_weight):
    tensor, data = lax.axis_index("tensor"), lax.axis_index("dp")
    x_hi, core = tensor % 2, data % 2
    z_mid = (data // 4) % 2
    place = jnp.stack([tensor // 2, x_hi, core, data // 16]).astype(jnp.int32)
    grad_scale = 1.0 / jnp.sqrt(jnp.float32(32768))
    clip_rows = clips.reshape(ROWS, 128)
    grads = out_grad.reshape(ROWS, 128)
    spatial = spatial_weight.reshape(9, 1024, 128)
    temporal = temporal_weight
    piece, wide_piece = shape((ROWS, 128), BF), shape((ROWS, 128), F32)

    cross = [
        (d * 8 + t, ((d + 16) % 32) * 8 + (t ^ 1)) for d in range(32) for t in range(8)
    ]
    (spatial_give,) = call(
        spatial_give_kernel, [shape((9, 2, 128, 128), BF)], [], [place, spatial], 0, "spatial_give"
    )
    (hidden_first,) = call(
        first_act_kernel, [piece], [], [clip_rows, spatial_give], 10**6, "first_act", unread=1
    )
    spatial_a = lax.ppermute(spatial_give, ("dp", "tensor"), cross)
    first_all = [hidden_first] + [tensor_move(hidden_first, d, 0) for d in (1, 2, 3)]
    (temporal_give,) = call(
        temporal_give_kernel,
        [shape((3, 2, 128, 128), BF)],
        [],
        [place, temporal, hidden_first],
        10**6,
        "temporal_give",
        unread=1,
    )
    spatial_a, temporal_give, grads, first_all = lax.optimization_barrier(
        (spatial_a, temporal_give, grads, first_all)
    )
    spatial_b = data_move(spatial_a, 1)
    grads_all = [grads] + [tensor_move(grads, d, 0) for d in (1, 2, 3)]
    temporal_a = lax.ppermute(temporal_give, ("dp", "tensor"), cross)
    out_scratch = [pltpu.VMEM((4608, 128), BF), pltpu.VMEM((8, 128, 4608), BF)]
    (out_give,) = call(
        spatial_partner_kernel,
        [piece],
        out_scratch,
        [place] + first_all + [spatial_a, spatial_b],
        ROWS * 4608 * 256,
        "spatial_partner",
    )
    temporal_a, out_give = lax.optimization_barrier((temporal_a, out_give))
    temporal_b = data_move(temporal_a, 1)
    temporal_args = [temporal, temporal_a, temporal_b]
    (out_own,) = call(
        spatial_own_kernel,
        [wide_piece],
        out_scratch,
        [place] + first_all + [spatial, out_give],
        ROWS * 4608 * 256,
        "spatial_own",
        unread=1,
    )
    out_got = tensor_move(out_give, 0, 1)
    (spatial_pair,) = call(
        spatial_pair_kernel,
        [shape((4608, 256), BF)],
        [],
        [place, spatial, spatial_a, spatial_b, out_give],
        10**6,
        "spatial_pair",
        unread=1,
    )
    second_own, second_give = call(
        grad_second_kernel,
        [wide_piece, piece],
        [pltpu.VMEM((3, 256, 512), BF), pltpu.VMEM((ROWS, 1536), BF)],
        [place] + grads_all + temporal_args + [out_give],
        2 * ROWS * 1536 * 256,
        "grad_second",
        unread=1,
    )
    second_got = tensor_move(second_give, 0, 1)
    (both,) = call(
        second_act_kernel,
        [shape((2, ROWS, 128), BF)],
        [],
        [out_own, out_got, second_own, second_got],
        10**7,
        "second_act",
    )
    both_pair = [both, tensor_move(both, 0, 1)]

    half = [shape((2, 8, 6, 32, 128), F32), shape((2, 8, 6, 32, 128), BF)]
    keep, give = call(
        early_grads_kernel,
        half,
        [
            pltpu.VMEM((512, ROWS), BF),
            pltpu.VMEM((8, 128, 1536), BF),
            pltpu.VMEM((512, 256), F32),
        ],
        [place] + first_all + both_pair + [spatial_pair],
        2 * ROWS * 1536 * 512,
        "early_grads",
        unread=1,
    )
    late_keep, late_give = call(
        late_grads_kernel,
        half,
        [
            pltpu.VMEM((512, ROWS), BF),
            pltpu.VMEM((512, ROWS), BF),
            pltpu.VMEM((8, 128, 768), BF),
            pltpu.VMEM((ROWS, 768), BF),
            pltpu.VMEM((512, 256), F32),
        ],
        [place] + first_all + grads_all + both_pair + [give],
        2 * ROWS * 1536 * 512,
        "late_grads",
        unread=1,
    )
    early_local = x_lo_sum(*core_sum(keep, give))
    own_back, own_ahead, *parts = call(
        both_back_kernel,
        [wide_piece, wide_piece] + [shape((2, ROWS, 128), BF)] * 3,
        [
            pltpu.VMEM((512, 2304), BF),
            pltpu.VMEM((8, 128, 2304), BF),
            pltpu.VMEM((3, 256, 512), BF),
            pltpu.VMEM((ROWS, 768), BF),
            pltpu.VMEM((256, 512), F32),
        ],
        [place] + both_pair + [spatial_pair] + temporal_args + [late_give],
        2 * ROWS * 3072 * 512,
        "both_back",
        unread=1,
    )

    late_local = x_lo_sum(*core_sum(late_keep, late_give))
    local = jnp.concatenate([early_local, late_local], axis=1)
    local, parts = lax.optimization_barrier((local, parts))
    parts = [tensor_move(parts[d - 1], d, 0) for d in (1, 2, 3)]
    local = lax.all_to_all(
        local,
        "dp",
        split_axis=0,
        concat_axis=0,
        tiled=True,
        axis_index_groups=Z_GROUPS,
    )
    share = (jnp.sum(local.astype(F32), axis=0) * grad_scale).astype(BF)
    move = []
    for d in range(32):
        for t in range(8):
            if (d // 4) % 2 != t % 2:
                move.append((d * 8 + t, (d ^ 4) * 8 + (t ^ 1)))
    moved = lax.ppermute(share, ("dp", "tensor"), move)
    share = jnp.where(z_mid == x_hi, share, moved)
    spatial_share = share[:9].reshape(3, 3, 32, 128)
    temporal_share = share[9:].swapaxes(1, 2)

    mixed, clip_grad = call(
        finish_kernel,
        [piece, piece],
        [],
        [clip_rows, grads, own_back, own_ahead] + parts,
        10**7,
        "finish",
    )
    return (
        mixed.reshape(clips.shape),
        clip_grad.reshape(clips.shape),
        spatial_share,
        temporal_share,
    )


def solution(mesh):
    placed = (
        P("dp", None, None, None, "tensor"),
        P("dp", None, None, None, "tensor"),
        P(None, None, None, "tensor"),
        P(None, "tensor", None),
    )
    return jax.shard_map(
        per_device,
        mesh=mesh,
        in_specs=placed,
        out_specs=(
            P("dp", None, None, None, "tensor"),
            P("dp", None, None, None, "tensor"),
            P(None, None, "dp", "tensor"),
            P(None, "tensor", "dp"),
        ),
        check_vma=False,
    )
```
